32 devices in a mesh: vocab: 4 (over z), hid: 4 (over y, x), tok: 2 (over core).
Axes of the slice: x: 2, y: 2, z: 4, core: 2. Of those that a mesh axis runs over, the one named last changes fastest.
Arguments:
- hidden: bfloat16 [1024, 8192], P('tok', ('hid', 'vocab')), may hold values from -300 to 300
- weight: bfloat16 [8192, 64128], P('hid', 'vocab'), may hold values from -0.1875 to 0.1875
- labels: int32 [1024], P('tok'), may hold values from 0 to 64127
Outputs:
- token_loss: float32 [1024], P('tok')
- mean_loss: float32 [], replicated
The draws below stay inside these ranges and needn't reach their ends.
All inputs are finite; a program needn't handle non-finite values.
Results may differ from the reference program's by a relative error of at most 0.0003.
Values may be sent and summed in bfloat16 or wider, within the bound.
A program may use at most 192 MiB of HBM per device.

```python
import jax
import jax.numpy as jnp
from jax import lax

D = 8192
V = 64128
TOK_DEV = 512
TOKENS = 1024


def draw_hidden(key, part):
    first, second = jax.random.split(jax.random.fold_in(key, 17), 2)
    values = jax.random.normal(first, (TOKENS, D), jnp.float32)
    scales = jnp.exp(jax.random.uniform(second, (TOKENS, 1), jnp.float32, jnp.log(0.5), jnp.log(4.0)))
    return jnp.clip(values * scales, -300.0, 300.0).astype(jnp.bfloat16)


def with_ends(drawn, rng, smallest, largest):
    index_at = [jax.random.randint(jax.random.fold_in(rng, axis), (), 0, length) for axis, length in enumerate(drawn.shape)]
    main_axis = drawn.shape.index(max(drawn.shape))
    next_to = index_at[:main_axis] + [(index_at[main_axis] + 1) % drawn.shape[main_axis]] + index_at[main_axis + 1:]
    return drawn.at[tuple(index_at)].set(smallest).at[tuple(next_to)].set(largest)


def shard_levels(own_key, dims, shards, low, high):
    def one(dim, parts):
        draws = jax.random.uniform(jax.random.fold_in(jax.random.fold_in(own_key, 6), dim), (parts,), jnp.float32, low / len(shards), high / len(shards))
        return jnp.repeat(jnp.exp(draws), dims[dim] // parts).reshape((-1,) + (1,) * (len(dims) - dim - 1))

    factor_of = one(*shards[0])
    for cut in shards[1:]:
        factor_of = factor_of * one(*cut)
    return factor_of


def centred(rng, shape, spread, limit, shards=(), held_as=jnp.bfloat16):
    result = jax.random.normal(rng, shape, jnp.float32) * spread
    if len(shards) > 0:
        result = shard_levels(rng, shape, shards, -0.22, 0.18) * result
    return jnp.clip(result, min=-limit, max=limit).astype(held_as)


def setup_inputs(seed: int = 0) -> dict:
    streams_of = jax.random.split(jax.random.key(seed), 4)
    return {
        "hidden": draw_hidden(jax.random.fold_in(streams_of[3], 71), 0),
        "weight": centred(streams_of[1], (D, V), (D // 9) ** -0.5, 0.1875, ((0, 4), (1, 4))),
        "labels": with_ends(jax.random.randint(streams_of[2], (TOKENS,), 0, V), jax.random.fold_in(streams_of[2], 1), 0, V - 1).astype(jnp.int32),
    }


def reference(hidden, weight, labels):
    hidden_blocks = hidden.reshape(TOKENS // TOK_DEV, TOK_DEV, D)
    label_blocks = labels.reshape(TOKENS // TOK_DEV, TOK_DEV)

    def one_block(pair):
        rows_in, label_rows = pair
        logits = jnp.dot(rows_in, weight, preferred_element_type=jnp.float32)
        row_top = jnp.max(logits, axis=1)
        lse = row_top + jnp.log(jnp.sum(jnp.exp(logits - row_top[:, None]), axis=1))
        target = jnp.take_along_axis(logits, label_rows[:, None].astype(jnp.int32), axis=1)[:, 0]
        return lse - target

    token_loss = lax.map(one_block, (hidden_blocks, label_blocks)).reshape(TOKENS)
    mean_loss = jnp.sum(token_loss) / TOKENS
    return token_loss, mean_loss
```

```python
import math

import jax
import jax.numpy as jnp
from jax import lax
from jax.sharding import PartitionSpec as P

CHUNKS = 3
ALIGN = 16
TOP_HIDDEN = 300.0
TOP_WEIGHT = 0.1875


def pieces(start, stop, count):
    step = -(-(stop - start) // count)
    step = -(-step // ALIGN) * ALIGN
    return [(at, min(at + step, stop)) for at in range(start, stop, step)]


def swap(x, bit, size):
    return lax.ppermute(x, "hid", [(i, i ^ bit) for i in range(size)])


def reduce_piece(hid_rel, weight_t, rows, first, second, scale, size):
    w = weight_t[rows[0]:rows[1]]
    third = first ^ second

    def part(index):
        picked = jnp.concatenate([hid_rel[i] for i in index], axis=0)
        return lax.dot_general(w, picked, (((1,), (1,)), ((), ())), preferred_element_type=jnp.float32)

    block = hid_rel[0].shape[0]
    sent = (part((first, third)) * scale).astype(jnp.float16)
    got = swap(sent, first, size)
    kept = part((0, second)) * scale + got.astype(jnp.float32)
    got2 = swap(kept[:, block:].astype(jnp.float16), second, size)
    return (kept[:, :block] + got2.astype(jnp.float32)) * (1.0 / scale)


def body(hidden, weight, labels):
    size = lax.axis_size("hid")
    me = lax.axis_index("hid")
    token_rows = hidden.shape[0]
    block = token_rows // size
    width = weight.shape[1]
    depth = hidden.shape[1] * size * lax.axis_size("vocab")
    scale = 2.0 ** -max(0, math.ceil(math.log2(depth * TOP_HIDDEN * TOP_WEIGHT / 65504.0)))
    weight_t = weight.T

    blocks = hidden.reshape(size, block, hidden.shape[1])
    rel = jnp.concatenate([lax.dynamic_index_in_dim(blocks, me ^ i, 0) for i in range(size)], axis=0)
    rel = lax.all_gather(rel, "vocab", axis=2, tiled=True)
    hid_rel = [rel[i] for i in range(size)]

    half = -(-(width // 2) // ALIGN) * ALIGN
    plan_a = [(p, 1, 2) for p in pieces(0, half, CHUNKS)]
    plan_b = [(p, 2, 1) for p in pieces(half, width, CHUNKS)]
    plan = [item for pair in zip(plan_a, plan_b) for item in pair]
    plan += plan_a[len(plan_b):] + plan_b[len(plan_a):]

    label_rows = lax.dynamic_slice_in_dim(labels, me * block, block, 0)
    shifted = label_rows - lax.axis_index("vocab") * width
    tops, sums, targets = [], [], []
    for rows, first, second in plan:
        logits = reduce_piece(hid_rel, weight_t, rows, first, second, scale, size)
        row_ids = lax.broadcasted_iota(jnp.int32, logits.shape, 0) + rows[0]
        top = jnp.max(logits, axis=0)
        tops.append(top)
        sums.append(jnp.sum(jnp.exp(logits - top[None]), axis=0))
        targets.append(jnp.sum(jnp.where(row_ids == shifted[None], logits, 0.0), axis=0))
    tops, sums = jnp.stack(tops), jnp.stack(sums)
    top = jnp.max(tops, axis=0)
    total = jnp.sum(sums * jnp.exp(tops - top[None]), axis=0)
    mine = jnp.stack([top, total, sum(targets)])

    every = lax.all_gather(mine, ("tok", "hid", "vocab"), axis=0, tiled=False)
    every = every.reshape(lax.axis_size("tok"), size, lax.axis_size("vocab"), 3, block)
    tops, sums, targets = every[..., 0, :], every[..., 1, :], every[..., 2, :]
    top = jnp.max(tops, axis=2)
    total = jnp.sum(sums * jnp.exp(tops - top[:, :, None]), axis=2)
    losses = top + jnp.log(total) - jnp.sum(targets, axis=2)
    losses = losses.reshape(lax.axis_size("tok"), token_rows)
    mean = jnp.sum(losses) / (token_rows * lax.axis_size("tok"))
    return lax.dynamic_index_in_dim(losses, lax.axis_index("tok"), 0, keepdims=False), mean


def solution(mesh):
    return jax.shard_map(
        body,
        mesh=mesh,
        in_specs=(P("tok", ("hid", "vocab")), P("hid", "vocab"), P("tok")),
        out_specs=(P("tok"), P()),
        check_vma=False,
    )
```

```python
import math

import jax
import jax.numpy as jnp
from jax import lax
from jax.sharding import PartitionSpec as P

CHUNKS = 6
WINDOW = 4
ALIGN = 16
TOP_HIDDEN = 300.0
TOP_WEIGHT = 0.1875


def pieces(start, stop, count):
    step = -(-(stop - start) // count)
    step = -(-step // ALIGN) * ALIGN
    return [(at, min(at + step, stop)) for at in range(start, stop, step)]


def swap(x, bit, size):
    return lax.ppermute(x, "hid", [(i, i ^ bit) for i in range(size)])


def send_piece(hid_rel, weight_t, rows, first, second, scale, size):
    w = weight_t[rows[0]:rows[1]]
    picked = jnp.concatenate([hid_rel[first], hid_rel[first ^ second]], axis=0)
    sent = lax.dot_general(w, picked, (((1,), (1,)), ((), ())), preferred_element_type=jnp.float32)
    return swap((sent * scale).astype(jnp.float16), first, size)


def sum_piece(hid_rel, weight_t, rows, got, second, scale, size):
    w = weight_t[rows[0]:rows[1]]
    block = hid_rel[0].shape[0]
    picked = jnp.concatenate([hid_rel[0], hid_rel[second]], axis=0)
    kept = lax.dot_general(w, picked, (((1,), (1,)), ((), ())), preferred_element_type=jnp.float32)
    kept = kept * scale + got.astype(jnp.float32)
    got2 = swap(kept[:, block:].astype(jnp.float16), second, size)
    return (kept[:, :block] + got2.astype(jnp.float32)) * (1.0 / scale)


def body(hidden, weight, labels):
    size = lax.axis_size("hid")
    me = lax.axis_index("hid")
    token_rows = hidden.shape[0]
    block = token_rows // size
    width = weight.shape[1]
    depth = hidden.shape[1] * size * lax.axis_size("vocab")
    scale = 2.0 ** -max(0, math.ceil(math.log2(depth * TOP_HIDDEN * TOP_WEIGHT / 65504.0)))
    weight_t = weight.T

    blocks = hidden.reshape(size, block, hidden.shape[1])
    hid_rel = {}
    for pair in ((1, 3), (2, 0)):
        rel = jnp.concatenate([lax.dynamic_index_in_dim(blocks, me ^ i, 0) for i in pair], axis=0)
        rel = lax.all_gather(rel, "vocab", axis=2, tiled=True)
        hid_rel[pair[0]], hid_rel[pair[1]] = rel[0], rel[1]

    half = -(-(width // 2) // ALIGN) * ALIGN
    plan_a = [(p, 1, 2) for p in pieces(0, half, CHUNKS)]
    plan_b = [(p, 2, 1) for p in pieces(half, width, CHUNKS)]
    plan = [item for pair in zip(plan_a, plan_b) for item in pair]
    plan += plan_a[len(plan_b):] + plan_b[len(plan_a):]

    got = []
    for index, (rows, first, second) in enumerate(plan):
        use = hid_rel
        if index >= WINDOW:
            use, got[index - WINDOW] = lax.optimization_barrier((hid_rel, got[index - WINDOW]))
        got.append(send_piece(use, weight_t, rows, first, second, scale, size))

    label_rows = lax.dynamic_slice_in_dim(labels, me * block, block, 0)
    shifted = label_rows - lax.axis_index("vocab") * width
    top = total = target = None
    for (rows, first, second), arrived in zip(plan, got):
        logits = sum_piece(hid_rel, weight_t, rows, arrived, second, scale, size)
        row_ids = lax.broadcasted_iota(jnp.int32, logits.shape, 0) + rows[0]
        new_top = jnp.max(logits, axis=0)
        if top is not None:
            new_top = jnp.maximum(top, new_top)
        part = jnp.sum(jnp.exp(logits - new_top[None]), axis=0)
        hit = jnp.sum(jnp.where(row_ids == shifted[None], logits, 0.0), axis=0)
        if top is not None:
            part, hit = total * jnp.exp(top - new_top) + part, target + hit
        top, total, target = new_top, part, hit

    every = lax.all_gather(jnp.stack([top, total, target]), "vocab", axis=0, tiled=False)
    tops, sums, targets = every[:, 0], every[:, 1], every[:, 2]
    top = jnp.max(tops, axis=0)
    total = jnp.sum(sums * jnp.exp(tops - top[None]), axis=0)
    losses = lax.all_gather(top + jnp.log(total) - jnp.sum(targets, axis=0), "hid", axis=0, tiled=True)
    loss_total = lax.psum(jnp.sum(losses), "tok")
    return losses, loss_total / (token_rows * lax.axis_size("tok"))


def solution(mesh):
    return jax.shard_map(
        body,
        mesh=mesh,
        in_specs=(P("tok", ("hid", "vocab")), P("hid", "vocab"), P("tok")),
        out_specs=(P("tok"), P()),
        check_vma=False,
    )
```

```python
import math

import jax
import jax.numpy as jnp
from jax import lax
from jax.sharding import PartitionSpec as P

CHUNKS = 6
WINDOW = 4
KEEP_AHEAD = 2
ALIGN = 16
TOP_HIDDEN = 300.0
TOP_WEIGHT = 0.1875


def pieces(start, stop, count):
    step = -(-(stop - start) // count)
    step = -(-step // ALIGN) * ALIGN
    return [(at, min(at + step, stop)) for at in range(start, stop, step)]


def swap(x, bit, size):
    return lax.ppermute(x, "hid", [(i, i ^ bit) for i in range(size)])


def send_piece(hid_rel, weight_t, rows, first, second, scale, size):
    w = weight_t[rows[0]:rows[1]]
    picked = jnp.concatenate([hid_rel[first], hid_rel[first ^ second]], axis=0)
    sent = lax.dot_general(w, picked, (((1,), (1,)), ((), ())), preferred_element_type=jnp.float32)
    return swap((sent * scale).astype(jnp.float16), first, size)


def sum_piece(hid_rel, weight_t, rows, got, second, scale, size):
    w = weight_t[rows[0]:rows[1]]
    block = hid_rel[0].shape[0]
    picked = jnp.concatenate([hid_rel[0], hid_rel[second]], axis=0)
    kept = lax.dot_general(w, picked, (((1,), (1,)), ((), ())), preferred_element_type=jnp.float32)
    kept = kept * scale + got.astype(jnp.float32)
    got2 = swap(kept[:, block:].astype(jnp.float16), second, size)
    return (kept[:, :block] + got2.astype(jnp.float32)) * (1.0 / scale)


def body(hidden, weight, labels):
    size = lax.axis_size("hid")
    me = lax.axis_index("hid")
    token_rows = hidden.shape[0]
    block = token_rows // size
    width = weight.shape[1]
    depth = hidden.shape[1] * size * lax.axis_size("vocab")
    scale = 2.0 ** -max(0, math.ceil(math.log2(depth * TOP_HIDDEN * TOP_WEIGHT / 65504.0)))
    weight_t = weight.T

    blocks = hidden.reshape(size, block, hidden.shape[1])
    rel = jnp.concatenate([lax.dynamic_index_in_dim(blocks, me ^ i, 0) for i in range(size)], axis=0)
    rel = lax.all_gather(rel, "vocab", axis=2, tiled=True)
    hid_rel = [rel[i] for i in range(size)]

    half = -(-(width // 2) // ALIGN) * ALIGN
    plan_a = [(p, 1, 2) for p in pieces(0, half, CHUNKS)]
    plan_b = [(p, 2, 1) for p in pieces(half, width, CHUNKS)]
    plan = [item for pair in zip(plan_a, plan_b) for item in pair]
    plan += plan_a[len(plan_b):] + plan_b[len(plan_a):]

    got = []
    for index, (rows, first, second) in enumerate(plan):
        use = hid_rel
        if index >= WINDOW:
            use, got[index - WINDOW] = lax.optimization_barrier((hid_rel, got[index - WINDOW]))
        got.append(send_piece(use, weight_t, rows, first, second, scale, size))

    label_rows = lax.dynamic_slice_in_dim(labels, me * block, block, 0)
    shifted = label_rows - lax.axis_index("vocab") * width
    top = total = target = None
    for index, (rows, first, second) in enumerate(plan):
        before = index if index < KEEP_AHEAD else index - KEEP_AHEAD
        use, got[before] = lax.optimization_barrier((hid_rel, got[before]))
        logits = sum_piece(use, weight_t, rows, got[index], second, scale, size)
        row_ids = lax.broadcasted_iota(jnp.int32, logits.shape, 0) + rows[0]
        new_top = jnp.max(logits, axis=0)
        if top is not None:
            new_top = jnp.maximum(top, new_top)
        part = jnp.sum(jnp.exp(logits - new_top[None]), axis=0)
        hit = jnp.sum(jnp.where(row_ids == shifted[None], logits, 0.0), axis=0)
        if top is not None:
            part, hit = total * jnp.exp(top - new_top) + part, target + hit
        top, total, target = new_top, part, hit

    every = lax.all_gather(jnp.stack([top, total, target]), "vocab", axis=0, tiled=False)
    tops, sums, targets = every[:, 0], every[:, 1], every[:, 2]
    top = jnp.max(tops, axis=0)
    total = jnp.sum(sums * jnp.exp(tops - top[None]), axis=0)
    losses = lax.all_gather(top + jnp.log(total) - jnp.sum(targets, axis=0), ("tok", "hid"), axis=0, tiled=True)
    own = lax.dynamic_slice_in_dim(losses, lax.axis_index("tok") * token_rows, token_rows, 0)
    return own, jnp.sum(losses) / losses.shape[0]


def solution(mesh):
    return jax.shard_map(
        body,
        mesh=mesh,
        in_specs=(P("tok", ("hid", "vocab")), P("hid", "vocab"), P("tok")),
        out_specs=(P("tok"), P()),
        check_vma=False,
    )
```

```python
import math

import jax
import jax.numpy as jnp
from jax import lax
from jax.sharding import PartitionSpec as P

CHUNKS = 6
WINDOW = 6
KEEP_AHEAD = 3
ALIGN = 16
TOP_HIDDEN = 300.0
TOP_WEIGHT = 0.1875


def pieces(start, stop, count):
    step = -(-(stop - start) // count)
    step = -(-step // ALIGN) * ALIGN
    return [(at, min(at + step, stop)) for at in range(start, stop, step)]


def swap(x, bit, size):
    return lax.ppermute(x, "hid", [(i, i ^ bit) for i in range(size)])


def send_piece(hid_rel, weight_t, rows, first, second, scale, size):
    w = weight_t[rows[0]:rows[1]]
    picked = jnp.concatenate([hid_rel[first], hid_rel[first ^ second]], axis=0)
    sent = lax.dot_general(w, picked, (((1,), (1,)), ((), ())), preferred_element_type=jnp.float32)
    return swap((sent * scale).astype(jnp.float16), first, size)


def sum_piece(hid_rel, weight_t, rows, got, second, scale, size):
    w = weight_t[rows[0]:rows[1]]
    block = hid_rel[0].shape[0]
    picked = jnp.concatenate([hid_rel[0], hid_rel[second]], axis=0)
    kept = lax.dot_general(w, picked, (((1,), (1,)), ((), ())), preferred_element_type=jnp.float32)
    kept = kept * scale + got.astype(jnp.float32)
    got2 = swap(kept[:, block:].astype(jnp.float16), second, size)
    return (kept[:, :block] + got2.astype(jnp.float32)) * (1.0 / scale)


def body(hidden, weight, labels):
    size = lax.axis_size("hid")
    me = lax.axis_index("hid")
    token_rows = hidden.shape[0]
    block = token_rows // size
    width = weight.shape[1]
    depth = hidden.shape[1] * size * lax.axis_size("vocab")
    scale = 2.0 ** -max(0, math.ceil(math.log2(depth * TOP_HIDDEN * TOP_WEIGHT / 65504.0)))
    weight_t = weight.T

    blocks = hidden.reshape(size, block, hidden.shape[1])
    rel = jnp.concatenate([lax.dynamic_index_in_dim(blocks, me ^ i, 0) for i in range(size)], axis=0)
    rel = lax.all_gather(rel, "vocab", axis=2, tiled=True)
    hid_rel = [rel[i] for i in range(size)]

    half = -(-(width // 2) // ALIGN) * ALIGN
    plan_a = [(p, 1, 2) for p in pieces(0, half, CHUNKS)]
    plan_b = [(p, 2, 1) for p in pieces(half, width, CHUNKS)]
    plan = [item for pair in zip(plan_a, plan_b) for item in pair]
    plan += plan_a[len(plan_b):] + plan_b[len(plan_a):]

    got = []
    for index, (rows, first, second) in enumerate(plan):
        use = hid_rel
        if index >= WINDOW:
            use, got[index - WINDOW] = lax.optimization_barrier((hid_rel, got[index - WINDOW]))
        got.append(send_piece(use, weight_t, rows, first, second, scale, size))

    label_rows = lax.dynamic_slice_in_dim(labels, me * block, block, 0)
    shifted = label_rows - lax.axis_index("vocab") * width
    top = total = target = None
    for index, (rows, first, second) in enumerate(plan):
        before = index if index < KEEP_AHEAD else index - KEEP_AHEAD
        use, got[before] = lax.optimization_barrier((hid_rel, got[before]))
        logits = sum_piece(use, weight_t, rows, got[index], second, scale, size)
        row_ids = lax.broadcasted_iota(jnp.int32, logits.shape, 0) + rows[0]
        new_top = jnp.max(logits, axis=0)
        if top is not None:
            new_top = jnp.maximum(top, new_top)
        part = jnp.sum(jnp.exp(logits - new_top[None]), axis=0)
        hit = jnp.sum(jnp.where(row_ids == shifted[None], logits, 0.0), axis=0)
        if top is not None:
            part, hit = total * jnp.exp(top - new_top) + part, target + hit
        top, total, target = new_top, part, hit

    every = lax.all_gather(jnp.stack([top, total, target]), "vocab", axis=0, tiled=False)
    tops, sums, targets = every[:, 0], every[:, 1], every[:, 2]
    top = jnp.max(tops, axis=0)
    total = jnp.sum(sums * jnp.exp(tops - top[None]), axis=0)
    losses = lax.all_gather(top + jnp.log(total) - jnp.sum(targets, axis=0), "hid", axis=0, tiled=True)
    loss_total = lax.psum(jnp.sum(losses), "tok")
    return losses, loss_total / (token_rows * lax.axis_size("tok"))


def solution(mesh):
    return jax.shard_map(
        body,
        mesh=mesh,
        in_specs=(P("tok", ("hid", "vocab")), P("hid", "vocab"), P("tok")),
        out_specs=(P("tok"), P()),
        check_vma=False,
    )
```
